32 devices in a mesh: seq: 16 (over z, y, x), head: 2 (over core).
Axes of the slice: x: 2, y: 2, z: 4, core: 2. Of those that a mesh axis runs over, the one named last changes fastest.
Arguments:
- inputs: bfloat16 [8192, 4096], P('seq', 'head'), may hold values from -6 to 6
- latent: float32 [4096, 512], P('seq', 'head'), as said below
- queries: bfloat16 [8192, 512], P('seq', 'head'), may hold values from -6 to 6
- keys: bfloat16 [8192, 512], P('seq', 'head'), may hold values from -6 to 6
- grad_out: bfloat16 [8192, 512], P('seq', 'head'), may hold values from -6 to 6
Outputs:
- attn_out: bfloat16 [8192, 512], P('seq', 'head')
- grad_queries: bfloat16 [8192, 512], P('seq', 'head')
- grad_keys: bfloat16 [8192, 512], P('seq', 'head')
- grad_latent: float32 [4096, 512], P('seq', 'head')
The draws below stay inside these ranges and needn't reach their ends.
Inputs may be any that keep to these rules, and one draw needn't show every extreme that they name: `latent`: no entry's magnitude lies between 0.67 and 1.5 times half of its column's mean magnitude.
All inputs are finite; a program needn't handle non-finite values.
Results may differ from the reference program's by a relative error of at most 0.014.
Values may be sent and summed in bfloat16 or wider, within the bound.
No kernel may reach another device: no remote copies, remote signals or barrier semaphores. Data moves between devices by JAX's collectives and lax.ppermute only.
A program may use at most 64 MiB of HBM per device.

```python
import math
import jax
import jax.numpy as jnp
from jax import lax

D = 4096
DK = 128
BLOCK = 128
HEADS = 4
TOKENS = 8192


def draw_latent(key, part):
    mixed_key = jax.random.fold_in(key, 11)
    key_band, key_small, key_large, key_sign, key_column = jax.random.split(mixed_key, 5)
    grid_shape = (D, HEADS * DK)
    share = 1.0 / 3.0
    banded = jax.random.uniform(key_band, grid_shape) < share
    small_size = jax.random.uniform(key_small, grid_shape, minval=0.02, maxval=0.2)
    large_size = jax.random.uniform(key_large, grid_shape, minval=0.7, maxval=1.5)
    ternary_signs = jnp.where(jax.random.bernoulli(key_sign, 0.5, grid_shape), 1.0, -1.0)
    column_base = jnp.exp(jax.random.uniform(key_column, (1, HEADS * DK), minval=math.log(0.5), maxval=math.log(2.0))) / math.sqrt(D)
    return (ternary_signs * jnp.where(banded, small_size, large_size) * column_base).astype(jnp.float32)


def level_of(own_key, shape, pieces, least, top_value):
    def one(axis_at, shards_of):
        heights = jax.random.uniform(jax.random.fold_in(jax.random.fold_in(own_key, 6), axis_at), (shards_of,), jnp.float32, least / len(pieces), top_value / len(pieces))
        return jnp.repeat(jnp.exp(heights), shape[axis_at] // shards_of).reshape((-1,) + (1,) * (len(shape) - axis_at - 1))

    level = one(*pieces[0])
    for cut in pieces[1:]:
        level = level * one(*cut)
    return level


def normal_values(stream_key, shape, spread, limit, pieces=(), dtype=jnp.bfloat16):
    result = spread * jax.random.normal(stream_key, shape, jnp.float32)
    if pieces:
        result = result * level_of(stream_key, shape, pieces, -0.22, 0.18)
    return jnp.clip(result, -limit, limit).astype(dtype)


def setup_inputs(seed: int = 0) -> dict:
    key_of = jax.random.split(jax.random.key(seed), 6)
    inputs = normal_values(key_of[0], (TOKENS, D), 1.0, 6.0, ((0, 16), (1, 2)))
    latent = draw_latent(jax.random.fold_in(key_of[5], 71), 0)
    queries = normal_values(key_of[2], (TOKENS, HEADS * DK), 1.0, 6.0, ((0, 16), (1, 2)))
    keys = normal_values(key_of[3], (TOKENS, HEADS * DK), 1.0, 6.0, ((0, 16), (1, 2)))
    grad_out = normal_values(key_of[4], (TOKENS, HEADS * DK), 1.0, 6.0, ((0, 16), (1, 2)))
    return dict(inputs=inputs, latent=latent, queries=queries, keys=keys, grad_out=grad_out)


absmean_eps = 1e-05
norm_eps = 1e-06

def ternarize(weights, column_scale):
    halfway = 0.5 * column_scale
    ternary_signs = jnp.where(weights > halfway, 1.0, jnp.where(weights < -halfway, -1.0, 0.0))
    return (ternary_signs * column_scale).astype(jnp.bfloat16)

def blocked(matrix):
    return matrix.reshape(TOKENS // BLOCK, BLOCK, HEADS, DK).astype(jnp.float32)

def rounded(matrix):
    return lax.optimization_barrier(matrix.astype(jnp.bfloat16)).astype(jnp.float32)

def reference(inputs, latent, queries, keys, grad_out):
    highest = lax.Precision.HIGHEST
    column_scale = lax.optimization_barrier(jnp.mean(jnp.abs(latent), axis=0)) + absmean_eps
    weights = ternarize(latent, column_scale)
    values_flat = jnp.dot(inputs, weights, preferred_element_type=jnp.float32)
    query_blocks = blocked(queries)
    key_blocks = blocked(keys)
    value_blocks = rounded(blocked(values_flat))
    causal = jnp.tril(jnp.ones((BLOCK, BLOCK), jnp.bool_))
    scores = rounded(jnp.where(causal, jnp.einsum('bthd,bshd->bhts', query_blocks, key_blocks, precision=highest), 0.0))
    within = jnp.einsum('bhts,bshd->bthd', scores, value_blocks, precision=highest)
    block_states = jnp.einsum('bshd,bshe->bhde', key_blocks, value_blocks, precision=highest)
    prior = jnp.cumsum(block_states, axis=0) - block_states
    across = jnp.einsum('bthd,bhde->bthe', query_blocks, prior, precision=highest)
    mixed = within + across
    root_mean = jnp.sqrt(lax.optimization_barrier(jnp.mean(mixed * mixed, axis=-1, keepdims=True)) + norm_eps)
    normed = mixed / root_mean
    attn_out = normed.astype(jnp.bfloat16).reshape(TOKENS, HEADS * DK)
    upstream = blocked(grad_out)
    inner_mean = lax.optimization_barrier(jnp.mean(upstream * normed, axis=-1, keepdims=True))
    grad_mixed = rounded((upstream - normed * inner_mean) / root_mean)
    grad_states = jnp.einsum('bthd,bthe->bhde', query_blocks, grad_mixed, precision=highest)
    following = lax.optimization_barrier(jnp.sum(grad_states, axis=0))[None] - jnp.cumsum(grad_states, axis=0)
    grad_scores = rounded(jnp.where(causal, jnp.einsum('bthe,bshe->bhts', grad_mixed, value_blocks, precision=highest), 0.0))
    grad_query = jnp.einsum('bhts,bshd->bthd', grad_scores, key_blocks, precision=highest) + jnp.einsum('bthe,bhde->bthd', grad_mixed, prior, precision=highest)
    grad_key = jnp.einsum('bhts,bthd->bshd', grad_scores, query_blocks, precision=highest) + jnp.einsum('bshe,bhde->bshd', value_blocks, following, precision=highest)
    grad_value = jnp.einsum('bhts,bthe->bshe', scores, grad_mixed, precision=highest) + jnp.einsum('bshd,bhde->bshe', key_blocks, following, precision=highest)
    grad_flat = grad_value.astype(jnp.bfloat16).reshape(TOKENS, HEADS * DK)
    grad_latent = lax.dot_general(inputs, grad_flat, (((0,), (0,)), ((), ())), preferred_element_type=jnp.float32)
    grad_queries = grad_query.astype(jnp.bfloat16).reshape(TOKENS, HEADS * DK)
    grad_keys = grad_key.astype(jnp.bfloat16).reshape(TOKENS, HEADS * DK)
    return (attn_out, grad_queries, grad_keys, grad_latent)
```

```python
import functools

import jax
import jax.numpy as jnp
from jax import lax
from jax.experimental import pallas as pl
from jax.experimental.pallas import tpu as pltpu
from jax.sharding import PartitionSpec as P

DK = 128
BLOCK = 128

absmean_eps = 1e-05
norm_eps = 1e-06

BF16 = jnp.bfloat16
F32 = jnp.float32
VMEM_LIMIT = 48 * 1024 * 1024


def rows_by_rows(a, b):
    return lax.dot_general(a, b, (((0,), (0,)), ((), ())), preferred_element_type=F32)


def by_rows(a, b):
    return lax.dot_general(a, b, (((1,), (1,)), ((), ())), preferred_element_type=F32)


def plain(a, b):
    return jnp.dot(a, b, preferred_element_type=F32)


def block_rows(i):
    return slice(i * BLOCK, (i + 1) * BLOCK)


def causal_mask():
    at = lax.broadcasted_iota(jnp.int32, (BLOCK, BLOCK), 0)
    of = lax.broadcasted_iota(jnp.int32, (BLOCK, BLOCK), 1)
    return at >= of


def place():
    s = lax.axis_index("seq")
    return lax.rem(s, 2), lax.div(s, 2), lax.axis_index("head")


def swap(array, axis, distance):
    count = lax.axis_size(axis)
    return lax.ppermute(array, axis, [(i, i ^ distance) for i in range(count)])


def project_kernel(slabs, heads, total_rows, *refs):
    slab_refs = refs[:slabs]
    sums_ref = refs[slabs]
    piece_refs = refs[slabs + 1 : slabs + 1 + 2 * heads]
    keep_ref, send_ref, x_ref, w_ref, sems = refs[slabs + 1 + 2 * heads :]
    side, pair, head = place()
    tokens, width = piece_refs[0].shape
    rows = slab_refs[0].shape[0]
    copies = []
    for k in range(heads):
        for t in range(2):
            at = pl.multiple_of((side ^ t) * tokens, tokens)
            lane = pl.multiple_of((head ^ k) * width, width)
            copy = pltpu.make_async_copy(
                piece_refs[2 * k + t],
                x_ref.at[pl.ds(at, tokens), pl.ds(lane, width)],
                sems.at[2 * k + t],
            )
            copy.start()
            copies.append(copy)
    scale = jnp.sum(sums_ref[...], axis=0, keepdims=True) / total_rows + absmean_eps
    halfway = 0.5 * scale
    for r in range(slabs):
        w = slab_refs[r][...].astype(F32)
        signs = jnp.where(w > halfway, scale, jnp.where(w < -halfway, -scale, 0.0))
        w_ref[pl.ds(pl.multiple_of((pair ^ r) * rows, rows), rows), :] = signs.astype(BF16)
    for copy in copies:
        copy.wait()
    step = 2 * BLOCK

    def one(i, carry):
        at = pl.ds(pl.multiple_of(i * step, step), step)
        p = plain(x_ref[at, :], w_ref[...])
        own = jnp.where(side == 0, p[:, :DK], p[:, DK:])
        other = jnp.where(side == 0, p[:, DK:], p[:, :DK])
        keep_ref[at, :] = own
        send_ref[at, :] = other.astype(BF16)
        return carry

    lax.fori_loop(0, 2 * tokens // step, one, 0)


def vmem_specs(n):
    return [pl.BlockSpec(memory_space=pltpu.VMEM)] * n


def call(kernel, outs, args, flops, scratch=(), specs=None):
    size = sum(a.size * a.dtype.itemsize for a in args)
    size += sum(o.size * o.dtype.itemsize for o in outs)
    return pl.pallas_call(
        kernel,
        out_shape=outs,
        in_specs=specs or vmem_specs(len(args)),
        out_specs=vmem_specs(len(outs)),
        scratch_shapes=list(scratch),
        compiler_params=pltpu.CompilerParams(vmem_limit_bytes=VMEM_LIMIT),
        cost_estimate=pl.CostEstimate(flops=flops, bytes_accessed=size, transcendentals=0),
    )(*args)


def shape(dims, dtype):
    return jax.ShapeDtypeStruct(dims, dtype)


def values_kernel(keep_ref, got_ref, k_ref, v_ref, total_ref, total16_ref):
    v = (keep_ref[...] + got_ref[...].astype(F32)).astype(BF16)
    v_ref[...] = v
    total = rows_by_rows(k_ref[...], v)
    total_ref[...] = total
    total16_ref[...] = total.astype(BF16)


def intra_kernel(blocks, q_ref, k_ref, v_ref, mixed_ref, local_ref):
    mask = causal_mask()
    state = jnp.zeros((DK, DK), F32)
    for i in range(blocks):
        q, k, v = (ref[block_rows(i), :] for ref in (q_ref, k_ref, v_ref))
        scores = jnp.where(mask, by_rows(q, k), 0.0).astype(BF16)
        earlier = state.astype(BF16)
        local_ref[i] = earlier
        mixed_ref[block_rows(i), :] = plain(scores, v) + plain(q, earlier)
        if i < blocks - 1:
            state = state + rows_by_rows(k, v)


def norm_kernel(mixed_ref, prior_ref, q_ref, up_ref, out_ref, gm_ref, total_ref, total16_ref):
    q = q_ref[...]
    mixed = mixed_ref[...] + plain(q, prior_ref[...].astype(BF16))
    inverse = lax.rsqrt(jnp.mean(mixed * mixed, axis=-1, keepdims=True) + norm_eps)
    normed = mixed * inverse
    out_ref[...] = normed.astype(BF16)
    up = up_ref[...].astype(F32)
    inner = jnp.mean(up * normed, axis=-1, keepdims=True)
    gm = ((up - normed * inner) * inverse).astype(BF16)
    gm_ref[...] = gm
    total = rows_by_rows(q, gm)
    total_ref[...] = total
    total16_ref[...] = total.astype(BF16)


def local_grad_kernel(
    blocks, q_ref, k_ref, v_ref, gm_ref, local_ref, prior_ref, gq_ref, gk_ref, gv_ref
):
    mask = causal_mask()
    state = jnp.zeros((DK, DK), F32)
    for i in reversed(range(blocks)):
        q, k, v, gm = (ref[block_rows(i), :] for ref in (q_ref, k_ref, v_ref, gm_ref))
        scores = jnp.where(mask, by_rows(q, k), 0.0).astype(BF16)
        gscores = jnp.where(mask, by_rows(gm, v), 0.0).astype(BF16)
        later = state.astype(BF16)
        prior = (prior_ref[...] + local_ref[i].astype(F32)).astype(BF16)
        gq_ref[block_rows(i), :] = (plain(gscores, k) + by_rows(gm, prior)).astype(BF16)
        gk_ref[block_rows(i), :] = rows_by_rows(gscores, q) + by_rows(v, later)
        gv_ref[block_rows(i), :] = rows_by_rows(scores, gm) + plain(k, later)
        if i:
            state = state + rows_by_rows(q, gm)


def grad_value_kernel(gv_ref, k_ref, after_ref, out_ref):
    out_ref[...] = (gv_ref[...] + plain(k_ref[...], after_ref[...].astype(BF16))).astype(BF16)


def grad_key_kernel(gk_ref, v_ref, after_ref, out_ref):
    out_ref[...] = (gk_ref[...] + by_rows(v_ref[...], after_ref[...].astype(BF16))).astype(BF16)


def latent_kernel(slabs, heads, *refs):
    own_ref, got_ref = refs[:2]
    piece_refs = refs[2 : 2 + 2 * heads]
    keep_ref, send_ref, x_ref, g_ref, sems = refs[2 + 2 * heads :]
    side, pair, head = place()
    tokens, width = piece_refs[0].shape
    copies = []
    for k in range(heads):
        for t in range(2):
            at = pl.multiple_of((side ^ t) * tokens, tokens)
            lane = pl.multiple_of((head ^ k) * width, width)
            copy = pltpu.make_async_copy(
                piece_refs[2 * k + t],
                x_ref.at[pl.ds(at, tokens), pl.ds(lane, width)],
                sems.at[2 * k + t],
            )
            copy.start()
            copies.append(copy)
    own, got = own_ref[...], got_ref[...]
    first = jnp.where(side == 0, own.astype(F32), got.astype(F32)).T.astype(BF16)
    second = jnp.where(side == 0, got.astype(F32), own.astype(F32)).T.astype(BF16)
    g_ref[:DK, :] = first
    g_ref[DK:, :] = second
    for copy in copies:
        copy.wait()
    rows = keep_ref.shape[-1]
    odd = lax.rem(pair, 2)
    for a in range(slabs):
        part = plain(g_ref[...], x_ref[:, a * rows : (a + 1) * rows])
        r = pair ^ a
        at = lax.div(r, 2)

        @pl.when(lax.rem(r, 2) == 0)
        def _():
            keep_ref[at] = part

        @pl.when(lax.rem(r, 2) == 1)
        def _():
            send_ref[at] = part.astype(BF16)


def sum_kernel(n, *refs):
    total = refs[0][...]
    for ref in refs[1:n]:
        total = total + ref[...].astype(F32)
    refs[n][...] = total.T


def pick(flag, even, odd):
    return jnp.where(flag == 0, even, odd)


def per_device(inputs, latent, queries, keys, grad_out):
    n, heads = lax.axis_size("seq"), lax.axis_size("head")
    side, pair, head = place()
    rows, columns = latent.shape
    tokens = inputs.shape[0]
    pairs, far = n // 2, n // 4
    blocks = 2 * tokens // BLOCK

    def half(flag):
        chunks = [
            pick(flag, inputs[:, 2 * c * rows :][:, :rows], inputs[:, (2 * c + 1) * rows :][:, :rows])
            for c in range(inputs.shape[1] // (2 * rows))
        ]
        return jnp.concatenate(chunks, axis=1)

    own_half = half(side)
    got_half = swap(half(1 - side), "seq", 1)
    pieces = [own_half, got_half]
    for k in range(1, heads):
        pieces += [swap(own_half, "head", k), swap(got_half, "head", k)]

    slab = latent.astype(BF16)
    sums = jnp.sum(jnp.abs(latent), axis=0)
    even = [slab] + [swap(slab, "seq", 4 * k) for k in range(1, far)]
    odd = [swap(a, "seq", 2) for a in even]
    slab_list = [a for two in zip(even, odd) for a in two]
    all_sums = lax.all_to_all(
        jnp.broadcast_to(sums[None], (n, columns)), "seq", 0, 0, tiled=True
    )

    def head_of(flag):
        return jnp.stack([pick(flag, a[:, :DK], a[:, DK:]) for a in (queries, keys, grad_out)])

    mine, theirs = head_of(side), swap(head_of(1 - side), "seq", 1)
    q, k, up = (
        jnp.concatenate([pick(side, mine[i], theirs[i]), pick(side, theirs[i], mine[i])], axis=0)
        for i in range(3)
    )

    any_specs = [pl.BlockSpec(memory_space=pl.ANY)] * len(pieces)
    keep, send = call(
        functools.partial(project_kernel, pairs, heads, n * rows),
        [shape((2 * tokens, DK), F32), shape((2 * tokens, DK), BF16)],
        slab_list + [all_sums] + pieces,
        2 * 2 * tokens * pairs * rows * columns,
        [
            pltpu.VMEM((2 * tokens, pairs * rows), BF16),
            pltpu.VMEM((pairs * rows, columns), BF16),
            pltpu.SemaphoreType.DMA((len(pieces),)),
        ],
        vmem_specs(pairs + 1) + any_specs,
    )
    long = 2 * tokens
    cost = 2 * long * DK * DK
    v, total, total16 = call(
        values_kernel,
        [shape((long, DK), BF16), shape((DK, DK), F32), shape((DK, DK), BF16)],
        [keep, swap(send, "seq", 1), k],
        cost,
    )

    def scan(total, total16, backward):
        before = jnp.zeros_like(total)
        distance = 1
        while distance < pairs:
            got = swap(total16, "seq", 2 * distance).astype(F32)
            high = lax.rem(lax.div(pair, distance), 2) == (0 if backward else 1)
            before = before + jnp.where(high, got, 0.0)
            total = total + got
            total16 = total.astype(BF16)
            distance *= 2
        return before

    prior = scan(total, total16, False)
    mixed, local = call(
        functools.partial(intra_kernel, blocks),
        [shape((long, DK), F32), shape((blocks, DK, DK), BF16)],
        [q, k, v],
        4 * cost,
    )
    out, gm, gtotal, gtotal16 = call(
        norm_kernel,
        [
            shape((long, DK), BF16),
            shape((long, DK), BF16),
            shape((DK, DK), F32),
            shape((DK, DK), BF16),
        ],
        [mixed, prior, q, up],
        2 * cost,
    )
    after = scan(gtotal, gtotal16, True)
    gq, gk_part, gv_part = call(
        functools.partial(local_grad_kernel, blocks),
        [shape((long, DK), BF16), shape((long, DK), F32), shape((long, DK), F32)],
        [q, k, v, gm, local, prior],
        9 * cost,
    )
    (gv,) = call(grad_value_kernel, [shape((long, DK), BF16)], [gv_part, k, after], cost)
    keep_parts, send_parts = call(
        functools.partial(latent_kernel, pairs, heads),
        [shape((far, columns, rows), F32), shape((far, columns, rows), BF16)],
        [gv, swap(gv, "seq", 1)] + pieces,
        2 * 2 * tokens * pairs * rows * columns,
        [
            pltpu.VMEM((2 * tokens, pairs * rows), BF16),
            pltpu.VMEM((columns, 2 * tokens), BF16),
            pltpu.SemaphoreType.DMA((len(pieces),)),
        ],
        vmem_specs(2) + any_specs,
    )
    (gk,) = call(grad_key_kernel, [shape((long, DK), BF16)], [gk_part, v, after], cost)

    arrived = []
    for i in reversed(range(1, far)):
        joined = keep_parts[i] + swap(send_parts[i], "seq", 2).astype(F32)
        arrived.append(swap(joined.astype(BF16), "seq", 4 * i))
    terms = [keep_parts[0], swap(send_parts[0], "seq", 2)] + arrived
    (grad_latent,) = call(
        functools.partial(sum_kernel, len(terms)), [shape((rows, columns), F32)], terms, 0
    )

    def token_half(flag):
        return jnp.stack([pick(flag, a[:tokens], a[tokens:]) for a in (out, gq, gk)])

    mine, theirs = token_half(side), swap(token_half(1 - side), "seq", 1)
    attn_out, grad_queries, grad_keys = (
        jnp.concatenate([pick(side, mine[i], theirs[i]), pick(side, theirs[i], mine[i])], axis=1)
        for i in range(3)
    )
    return (attn_out, grad_queries, grad_keys, grad_latent)


def solution(mesh):
    placed = (P("seq", "head"),) * 5
    return jax.shard_map(
        per_device,
        mesh=mesh,
        in_specs=placed,
        out_specs=(P("seq", "head"),) * 4,
        check_vma=False,
    )
```

```python
import functools

import jax
import jax.numpy as jnp
from jax import lax
from jax.experimental import pallas as pl
from jax.experimental.pallas import tpu as pltpu
from jax.sharding import PartitionSpec as P

DK = 128
BLOCK = 128

absmean_eps = 1e-05
norm_eps = 1e-06

BF16 = jnp.bfloat16
F32 = jnp.float32
VMEM_LIMIT = 20 * 1024 * 1024


def rows_by_rows(a, b):
    return lax.dot_general(a, b, (((0,), (0,)), ((), ())), preferred_element_type=F32)


def by_rows(a, b):
    return lax.dot_general(a, b, (((1,), (1,)), ((), ())), preferred_element_type=F32)


def plain(a, b):
    return jnp.dot(a, b, preferred_element_type=F32)


def block_rows(i):
    return slice(i * BLOCK, (i + 1) * BLOCK)


def causal_mask():
    at = lax.broadcasted_iota(jnp.int32, (BLOCK, BLOCK), 0)
    of = lax.broadcasted_iota(jnp.int32, (BLOCK, BLOCK), 1)
    return at >= of


def place():
    s = lax.axis_index("seq")
    return lax.rem(s, 2), lax.div(s, 2), lax.axis_index("head")


def swap(array, axis, distance):
    count = lax.axis_size(axis)
    return lax.ppermute(array, axis, [(i, i ^ distance) for i in range(count)])


EXTRA = 16


def slab_kernel(latent_ref, sums_ref, got_ref, out_ref):
    rows, columns = latent_ref.shape
    out_ref[:rows, :] = latent_ref[...].astype(BF16)
    rest = sums_ref[...] + got_ref[...]
    row = lax.broadcasted_iota(jnp.int32, (EXTRA, columns), 0)
    tail = jnp.zeros((EXTRA, columns), F32)
    for i in range(3):
        part = rest.astype(BF16).astype(F32)
        tail = jnp.where(row == i, part, tail)
        rest = rest - part
    out_ref[rows:, :] = tail.astype(BF16)


def project(piece_refs, w_ref, keep_ref, send_ref):
    side, _, head = place()
    width = piece_refs[0].shape[1]
    p = None
    for k, ref in enumerate(piece_refs):
        part = w_ref[pl.ds(pl.multiple_of((head ^ k) * width, width), width), :]
        term = plain(ref[...], part)
        p = term if p is None else p + term
    keep_ref[...] = jnp.where(side == 0, p[:, :DK], p[:, DK:])
    send_ref[...] = jnp.where(side == 0, p[:, DK:], p[:, :DK]).astype(BF16)


def project_own_kernel(far, slabs, total_rows, *refs):
    slab_refs, piece_refs = refs[:slabs], refs[slabs:-5]
    w_ref, keep_ref, send_ref, slabs_ref, sems = refs[-5:]
    copies = [
        pltpu.make_async_copy(a, slabs_ref.at[i], sems.at[i]) for i, a in enumerate(slab_refs)
    ]
    for copy in copies:
        copy.start()
    for copy in copies:
        copy.wait()
    _, pair, _ = place()
    rows = slab_refs[0].shape[0] - EXTRA
    sums = jnp.sum(slabs_ref[:, rows:, :].astype(F32), axis=0)
    scale = jnp.sum(sums, axis=0, keepdims=True) / total_rows + absmean_eps
    halfway = 0.5 * scale
    for i in range(slabs):
        r = 2 * i if i < far else 2 * (i - far) + 1
        w = slabs_ref[i, :rows, :].astype(F32)
        signs = jnp.where(w > halfway, scale, jnp.where(w < -halfway, -scale, 0.0))
        w_ref[pl.ds(pl.multiple_of((pair ^ r) * rows, rows), rows), :] = signs.astype(BF16)
    project(piece_refs, w_ref, keep_ref, send_ref)


def project_got_kernel(w_ref, *refs):
    project(refs[:-2], w_ref, *refs[-2:])


def park_kernel(n, *refs):
    copies = [pltpu.make_async_copy(refs[i], refs[n + 1 + i], refs[-1].at[i]) for i in range(n)]
    for copy in copies:
        copy.start()
    for copy in copies:
        copy.wait()


def park(arrays, after):
    n = len(arrays)
    return pl.pallas_call(
        functools.partial(park_kernel, n),
        out_shape=[pltpu.HBM(a.shape, a.dtype) for a in arrays],
        in_specs=vmem_specs(n) + [pl.BlockSpec(memory_space=pl.ANY)],
        out_specs=[pl.BlockSpec(memory_space=pltpu.HBM)] * n,
        scratch_shapes=[pltpu.SemaphoreType.DMA((n,))],
        compiler_params=pltpu.CompilerParams(vmem_limit_bytes=VMEM_LIMIT),
    )(*arrays, after)


def vmem_specs(n):
    return [pl.BlockSpec(memory_space=pltpu.VMEM)] * n


def call(kernel, outs, args, flops, scratch=(), specs=None):
    size = sum(a.size * a.dtype.itemsize for a in args)
    size += sum(o.size * o.dtype.itemsize for o in outs)
    return pl.pallas_call(
        kernel,
        out_shape=outs,
        in_specs=specs or vmem_specs(len(args)),
        out_specs=vmem_specs(len(outs)),
        scratch_shapes=list(scratch),
        compiler_params=pltpu.CompilerParams(vmem_limit_bytes=VMEM_LIMIT),
        cost_estimate=pl.CostEstimate(flops=flops, bytes_accessed=size, transcendentals=0),
    )(*args)


def shape(dims, dtype):
    return jax.ShapeDtypeStruct(dims, dtype)


def values_kernel(own_ref, own_got_ref, got_ref, got_got_ref, k_ref, v_ref, total_ref, total16_ref):
    side, _, _ = place()
    tokens = own_ref.shape[0]
    own = (own_ref[...] + own_got_ref[...].astype(F32)).astype(BF16)
    got = (got_ref[...] + got_got_ref[...].astype(F32)).astype(BF16)
    v_ref[pl.ds(pl.multiple_of(side * tokens, tokens), tokens), :] = own
    v_ref[pl.ds(pl.multiple_of((1 - side) * tokens, tokens), tokens), :] = got
    total = rows_by_rows(k_ref[...], v_ref[...])
    total_ref[...] = total
    total16_ref[...] = total.astype(BF16)


def intra_kernel(blocks, q_ref, k_ref, v_ref, mixed_ref, local_ref):
    mask = causal_mask()
    state = jnp.zeros((DK, DK), F32)
    for i in range(blocks):
        q, k, v = (ref[block_rows(i), :] for ref in (q_ref, k_ref, v_ref))
        scores = jnp.where(mask, by_rows(q, k), 0.0).astype(BF16)
        earlier = state.astype(BF16)
        local_ref[i] = earlier
        mixed_ref[block_rows(i), :] = plain(scores, v) + plain(q, earlier)
        if i < blocks - 1:
            state = state + rows_by_rows(k, v)


def norm_kernel(mixed_ref, prior_ref, q_ref, up_ref, out_ref, gm_ref, total_ref, total16_ref):
    q = q_ref[...]
    mixed = mixed_ref[...] + plain(q, prior_ref[...].astype(BF16))
    inverse = lax.rsqrt(jnp.mean(mixed * mixed, axis=-1, keepdims=True) + norm_eps)
    normed = mixed * inverse
    out_ref[...] = normed.astype(BF16)
    up = up_ref[...].astype(F32)
    inner = jnp.mean(up * normed, axis=-1, keepdims=True)
    gm = ((up - normed * inner) * inverse).astype(BF16)
    gm_ref[...] = gm
    total = rows_by_rows(q, gm)
    total_ref[...] = total
    total16_ref[...] = total.astype(BF16)


def local_grad_kernel(
    blocks, q_ref, k_ref, v_ref, gm_ref, local_ref, prior_ref, gq_ref, gk_ref, gv_ref, gv16_ref
):
    mask = causal_mask()
    state = jnp.zeros((DK, DK), F32)
    for i in reversed(range(blocks)):
        q, k, v, gm = (ref[block_rows(i), :] for ref in (q_ref, k_ref, v_ref, gm_ref))
        scores = jnp.where(mask, by_rows(q, k), 0.0).astype(BF16)
        gscores = jnp.where(mask, by_rows(gm, v), 0.0).astype(BF16)
        later = state.astype(BF16)
        prior = (prior_ref[...] + local_ref[i].astype(F32)).astype(BF16)
        gq_ref[block_rows(i), :] = (plain(gscores, k) + by_rows(gm, prior)).astype(BF16)
        gk_ref[block_rows(i), :] = rows_by_rows(gscores, q) + by_rows(v, later)
        gv = rows_by_rows(scores, gm) + plain(k, later)
        gv_ref[block_rows(i), :] = gv
        gv16_ref[block_rows(i), :] = gv.astype(BF16)
        if i:
            state = state + rows_by_rows(q, gm)


def grad_key_kernel(gk_ref, v_ref, after_ref, out_ref):
    out_ref[...] = (gk_ref[...] + by_rows(v_ref[...], after_ref[...])).astype(BF16)


def latent_part(sent, piece_refs, g_ref, out_ref):
    _, pair, head = place()
    width = piece_refs[0].shape[1]
    rows = out_ref.shape[-1]
    chunks = width // rows
    odd = lax.rem(pair, 2) ^ sent
    for k in range(len(piece_refs) // 2):
        for c in range(0, chunks, 2):
            part = None
            for t in range(2):
                two = piece_refs[2 * k + t][:, c * rows : (c + 2) * rows]
                one = jnp.where(odd == 0, two[:, :rows], two[:, rows:])
                term = plain(g_ref[t], one)
                part = term if part is None else part + term
            slab = (head ^ k) * chunks + c + odd
            out_ref[lax.div(pair ^ slab, 2)] = part.astype(out_ref.dtype)


def latent_send_kernel(gv_ref, k_ref, after_ref, got_ref, k_got_ref, after_got_ref, *refs):
    piece_refs = refs[:-2]
    out_ref, g_ref = refs[-2:]
    side, _, _ = place()
    tokens = piece_refs[0].shape[0]
    after, after_got = after_ref[...], after_got_ref[...]
    for t in range(2):
        at = pl.ds(pl.multiple_of((side ^ t) * tokens, tokens), tokens)
        own = gv_ref[at, :] + plain(k_ref[at, :], after)
        got = got_ref[at, :].astype(F32) + plain(k_got_ref[at, :], after_got)
        g_ref[t, :DK, :] = jnp.where(side == 0, own, got).T.astype(BF16)
        g_ref[t, DK:, :] = jnp.where(side == 0, got, own).T.astype(BF16)
    latent_part(1, piece_refs, g_ref, out_ref)


def latent_keep_kernel(g_ref, *refs):
    latent_part(0, refs[:-1], g_ref, refs[-1])


def join_kernel(i, keep_ref, got_ref, out_ref):
    out_ref[...] = (keep_ref[i] + got_ref[...].astype(F32)).astype(BF16)


def sum_kernel(n, *refs):
    total = refs[0][0]
    for ref in refs[1:n]:
        total = total + ref[...].astype(F32)
    refs[n][...] = total.T


def in_hbm(array):
    return pltpu.with_memory_space_constraint(array, pltpu.HBM)


def pick(flag, even, odd):
    return jnp.where(flag == 0, even, odd)


def per_device(inputs, latent, queries, keys, grad_out):
    n, heads = lax.axis_size("seq"), lax.axis_size("head")
    side, pair, head = place()
    rows, columns = latent.shape
    tokens = inputs.shape[0]
    pairs, far = n // 2, n // 4
    blocks = 2 * tokens // BLOCK

    def half(flag):
        chunks = [
            pick(flag, inputs[:, 2 * c * rows :][:, :rows], inputs[:, (2 * c + 1) * rows :][:, :rows])
            for c in range(inputs.shape[1] // (2 * rows))
        ]
        return jnp.concatenate(chunks, axis=1)

    sums = jnp.sum(jnp.abs(latent), axis=0, keepdims=True)
    got_sums = swap(sums, "seq", 1)
    sent_half, got_sums = lax.optimization_barrier((half(1 - side), got_sums))
    got_half = swap(sent_half, "seq", 1)
    own_half = half(side)

    (slab,) = call(slab_kernel, [shape((rows + EXTRA, columns), BF16)], [latent, sums, got_sums], 0)
    even = [slab] + [None] * (far - 1)
    odd = [swap(slab, "seq", 2)] + [None] * (far - 1)
    for i in range(2, far):
        even[i] = swap(slab, "seq", 4 * i)
    even[2:], odd[0], slab_late = lax.optimization_barrier((even[2:], odd[0], slab))
    for i in range(2, far):
        odd[i] = swap(even[i], "seq", 2)
    if far > 1:
        even[1] = swap(slab_late, "seq", 4)
        odd[1] = swap(even[1], "seq", 2)
    slab_list = even + odd
    own_late, _ = lax.optimization_barrier((own_half, even[-1]))
    own_pieces = [own_half] + [swap(own_late, "head", k) for k in range(1, heads)]
    half_cost = 2 * tokens * pairs * rows * columns
    weights, keep_own, send_own = call(
        functools.partial(project_own_kernel, far, len(slab_list), n * rows),
        [
            shape((pairs * rows, columns), BF16),
            shape((tokens, DK), F32),
            shape((tokens, DK), BF16),
        ],
        [in_hbm(a) for a in slab_list] + own_pieces,
        half_cost,
        [pltpu.VMEM((pairs, *slab.shape), BF16), pltpu.SemaphoreType.DMA((pairs,))],
        [pl.BlockSpec(memory_space=pl.ANY)] * pairs + vmem_specs(heads),
    )
    got_late, _ = lax.optimization_barrier((got_half, odd))
    keys_late, _ = lax.optimization_barrier((keys, even[-1]))
    got_pieces = [got_half] + [swap(got_late, "head", k) for k in range(1, heads)]
    keep_got, send_got = call(
        project_got_kernel,
        [shape((tokens, DK), F32), shape((tokens, DK), BF16)],
        [weights] + got_pieces,
        half_cost,
    )
    values_got, values_own = swap(send_own, "seq", 1), swap(send_got, "seq", 1)
    pieces = [a for two in zip(own_pieces, got_pieces) for a in two]

    def part_of(array, flag):
        return pick(flag, array[:, :DK], array[:, DK:])

    def joined(mine, theirs, late):
        mine, theirs, _ = lax.optimization_barrier((mine, theirs, late))
        return jnp.concatenate([pick(side, mine, theirs), pick(side, theirs, mine)], axis=0)

    k = joined(part_of(keys_late, side), swap(part_of(keys_late, 1 - side), "seq", 1), send_got)
    long = 2 * tokens
    cost = 2 * long * DK * DK
    v, total, total16 = call(
        values_kernel,
        [shape((long, DK), BF16), shape((DK, DK), F32), shape((DK, DK), BF16)],
        [keep_own, values_own, keep_got, values_got, k],
        cost,
    )
    parked = list(park(pieces, v))
    queries_late, up_late, keys_later, _ = lax.optimization_barrier(
        (queries, grad_out, keys, send_got)
    )
    early = [
        (part_of(a, side), swap(part_of(a, 1 - side), "seq", 1)) for a in (queries_late, up_late)
    ]
    k_parts = part_of(keys_later, 1 - side), swap(part_of(keys_later, side), "seq", 1)

    def scan(total, total16, backward, hooks):
        before = jnp.zeros_like(total)
        distance, at, results = 1, 0, []
        while distance < pairs:
            got = swap(total16, "seq", 2 * distance).astype(F32)
            high = lax.rem(lax.div(pair, distance), 2) == (0 if backward else 1)
            before = before + jnp.where(high, got, 0.0)
            if at < len(hooks):
                result = hooks[at](total16)
            total = total + got
            total16 = total.astype(BF16)
            if at < len(hooks):
                total16, result = lax.optimization_barrier((total16, result))
                results.append(result)
            distance, at = distance * 2, at + 1
        return before, results

    def intra():
        return call(
            functools.partial(intra_kernel, blocks),
            [shape((long, DK), F32), shape((blocks, DK, DK), BF16)],
            [q, k, v],
            4 * cost,
        )

    prior, (pieces, (q, up)) = scan(
        total,
        total16,
        False,
        [lambda _: parked, lambda late: [joined(*a, late) for a in early]],
    )
    mixed, local_prior = intra()
    out, gm, gtotal, gtotal16 = call(
        norm_kernel,
        [
            shape((long, DK), BF16),
            shape((long, DK), BF16),
            shape((DK, DK), F32),
            shape((DK, DK), BF16),
        ],
        [mixed, prior, q, up],
        2 * cost,
    )

    def local_grads():
        return call(
            functools.partial(local_grad_kernel, blocks),
            [
                shape((long, DK), BF16),
                shape((long, DK), F32),
                shape((long, DK), F32),
                shape((long, DK), BF16),
            ],
            [q, k, v, gm, local_prior, prior],
            9 * cost,
        )

    local = local_grads()
    after, ((_, (gq, gk_part, gv_part, gv16)), k_got) = scan(
        gtotal, gtotal16, True, [lambda _: ((), local), lambda late: joined(*k_parts, late)]
    )
    gv_got = swap(gv16, "seq", 1)
    after16 = after.astype(BF16)
    after16, gv_got = lax.optimization_barrier((after16, gv_got))
    after_got = swap(after16, "seq", 1)
    half_slabs = (far, columns, rows)
    send_parts, gv_both = call(
        latent_send_kernel,
        [shape(half_slabs, BF16), shape((2, columns, tokens), BF16)],
        [gv_part, k, after16, gv_got, k_got, after_got] + pieces,
        half_cost + 2 * cost,
    )
    (keep_parts,) = call(
        latent_keep_kernel, [shape(half_slabs, F32)], [gv_both] + pieces, half_cost
    )
    after_late, _ = lax.optimization_barrier((after16, send_parts))
    (gk,) = call(grad_key_kernel, [shape((long, DK), BF16)], [gk_part, v, after_late], cost)

    arrived = []
    for i in reversed(range(1, far)):
        (joined,) = call(
            functools.partial(join_kernel, i),
            [shape((columns, rows), BF16)],
            [keep_parts, swap(send_parts[i], "seq", 2)],
            0,
        )
        arrived.append(swap(joined, "seq", 4 * i))
    terms = [keep_parts, swap(send_parts[0], "seq", 2)] + arrived
    def token_half(flag):
        return jnp.stack([pick(flag, a[:tokens], a[tokens:]) for a in (out, gq, gk)])

    mine, theirs = token_half(side), swap(token_half(1 - side), "seq", 1)
    attn_out, grad_queries, grad_keys = (
        jnp.concatenate([pick(side, mine[i], theirs[i]), pick(side, theirs[i], mine[i])], axis=1)
        for i in range(3)
    )
    outs, terms = lax.optimization_barrier(((attn_out, grad_queries, grad_keys), terms))
    (grad_latent,) = call(
        functools.partial(sum_kernel, len(terms)), [shape((rows, columns), F32)], terms, 0
    )
    return (*outs, grad_latent)


def solution(mesh):
    placed = (P("seq", "head"),) * 5
    return jax.shard_map(
        per_device,
        mesh=mesh,
        in_specs=placed,
        out_specs=(P("seq", "head"),) * 4,
        check_vma=False,
    )
```

```python
import functools

import jax
import jax.numpy as jnp
from jax import lax
from jax.experimental import pallas as pl
from jax.experimental.pallas import tpu as pltpu
from jax.sharding import PartitionSpec as P

DK = 128
BLOCK = 128

absmean_eps = 1e-05
norm_eps = 1e-06

BF16 = jnp.bfloat16
F32 = jnp.float32
VMEM_LIMIT = 20 * 1024 * 1024


def rows_by_rows(a, b):
    return lax.dot_general(a, b, (((0,), (0,)), ((), ())), preferred_element_type=F32)


def by_rows(a, b):
    return lax.dot_general(a, b, (((1,), (1,)), ((), ())), preferred_element_type=F32)


def plain(a, b):
    return jnp.dot(a, b, preferred_element_type=F32)


def block_rows(i):
    return slice(i * BLOCK, (i + 1) * BLOCK)


def causal_mask():
    at = lax.broadcasted_iota(jnp.int32, (BLOCK, BLOCK), 0)
    of = lax.broadcasted_iota(jnp.int32, (BLOCK, BLOCK), 1)
    return at >= of


def place():
    s = lax.axis_index("seq")
    return lax.rem(s, 2), lax.div(s, 2), lax.axis_index("head")


def swap(array, axis, distance):
    count = lax.axis_size(axis)
    return lax.ppermute(array, axis, [(i, i ^ distance) for i in range(count)])


EXTRA = 16


def slab_kernel(latent_ref, sums_ref, got_ref, out_ref):
    rows, columns = latent_ref.shape
    out_ref[:rows, :] = latent_ref[...].astype(BF16)
    rest = sums_ref[...] + got_ref[...]
    row = lax.broadcasted_iota(jnp.int32, (EXTRA, columns), 0)
    tail = jnp.zeros((EXTRA, columns), F32)
    for i in range(3):
        part = rest.astype(BF16).astype(F32)
        tail = jnp.where(row == i, part, tail)
        rest = rest - part
    out_ref[rows:, :] = tail.astype(BF16)


def project(piece_refs, w_ref, keep_ref, send_ref):
    side, _, head = place()
    width = piece_refs[0].shape[1]
    p = None
    for k, ref in enumerate(piece_refs):
        part = w_ref[pl.ds(pl.multiple_of((head ^ k) * width, width), width), :]
        term = plain(ref[...], part)
        p = term if p is None else p + term
    keep_ref[...] = jnp.where(side == 0, p[:, :DK], p[:, DK:])
    send_ref[...] = jnp.where(side == 0, p[:, DK:], p[:, :DK]).astype(BF16)


def project_own_kernel(far, slabs, total_rows, *refs):
    slab_refs, piece_refs = refs[:slabs], refs[slabs:-5]
    w_ref, keep_ref, send_ref, slabs_ref, sems = refs[-5:]
    copies = [
        pltpu.make_async_copy(a, slabs_ref.at[i], sems.at[i]) for i, a in enumerate(slab_refs)
    ]
    for copy in copies:
        copy.start()
    for copy in copies:
        copy.wait()
    _, pair, _ = place()
    rows = slab_refs[0].shape[0] - EXTRA
    sums = jnp.sum(slabs_ref[:, rows:, :].astype(F32), axis=0)
    scale = jnp.sum(sums, axis=0, keepdims=True) / total_rows + absmean_eps
    halfway = 0.5 * scale
    for i in range(slabs):
        r = 2 * i if i < far else 2 * (i - far) + 1
        w = slabs_ref[i, :rows, :].astype(F32)
        signs = jnp.where(w > halfway, scale, jnp.where(w < -halfway, -scale, 0.0))
        w_ref[pl.ds(pl.multiple_of((pair ^ r) * rows, rows), rows), :] = signs.astype(BF16)
    project(piece_refs, w_ref, keep_ref, send_ref)


def project_got_kernel(w_ref, *refs):
    project(refs[:-2], w_ref, *refs[-2:])


def park_kernel(n, *refs):
    copies = [pltpu.make_async_copy(refs[i], refs[n + 1 + i], refs[-1].at[i]) for i in range(n)]
    for copy in copies:
        copy.start()
    for copy in copies:
        copy.wait()


def park(arrays, after):
    n = len(arrays)
    return pl.pallas_call(
        functools.partial(park_kernel, n),
        out_shape=[pltpu.HBM(a.shape, a.dtype) for a in arrays],
        in_specs=vmem_specs(n) + [pl.BlockSpec(memory_space=pl.ANY)],
        out_specs=[pl.BlockSpec(memory_space=pltpu.HBM)] * n,
        scratch_shapes=[pltpu.SemaphoreType.DMA((n,))],
        compiler_params=pltpu.CompilerParams(vmem_limit_bytes=VMEM_LIMIT),
    )(*arrays, after)


def vmem_specs(n):
    return [pl.BlockSpec(memory_space=pltpu.VMEM)] * n


def call(kernel, outs, args, flops, scratch=(), specs=None):
    size = sum(a.size * a.dtype.itemsize for a in args)
    size += sum(o.size * o.dtype.itemsize for o in outs)
    return pl.pallas_call(
        kernel,
        out_shape=outs,
        in_specs=specs or vmem_specs(len(args)),
        out_specs=vmem_specs(len(outs)),
        scratch_shapes=list(scratch),
        compiler_params=pltpu.CompilerParams(vmem_limit_bytes=VMEM_LIMIT),
        cost_estimate=pl.CostEstimate(flops=flops, bytes_accessed=size, transcendentals=0),
    )(*args)


def shape(dims, dtype):
    return jax.ShapeDtypeStruct(dims, dtype)


def values_kernel(own_ref, own_got_ref, got_ref, got_got_ref, k_ref, v_ref, total_ref, total16_ref):
    side, _, _ = place()
    tokens = own_ref.shape[0]
    own = (own_ref[...] + own_got_ref[...].astype(F32)).astype(BF16)
    got = (got_ref[...] + got_got_ref[...].astype(F32)).astype(BF16)
    v_ref[pl.ds(pl.multiple_of(side * tokens, tokens), tokens), :] = own
    v_ref[pl.ds(pl.multiple_of((1 - side) * tokens, tokens), tokens), :] = got
    total = rows_by_rows(k_ref[...], v_ref[...])
    total_ref[...] = total
    total16_ref[...] = total.astype(BF16)


def intra_kernel(blocks, q_ref, k_ref, v_ref, mixed_ref, local_ref):
    mask = causal_mask()
    state = jnp.zeros((DK, DK), F32)
    for i in range(blocks):
        q, k, v = (ref[block_rows(i), :] for ref in (q_ref, k_ref, v_ref))
        scores = jnp.where(mask, by_rows(q, k), 0.0).astype(BF16)
        earlier = state.astype(BF16)
        local_ref[i] = earlier
        mixed_ref[block_rows(i), :] = plain(scores, v) + plain(q, earlier)
        if i < blocks - 1:
            state = state + rows_by_rows(k, v)


def norm_kernel(mixed_ref, prior_ref, q_ref, up_ref, out_ref, gm_ref, total_ref, total16_ref):
    q = q_ref[...]
    mixed = mixed_ref[...] + plain(q, prior_ref[...].astype(BF16))
    inverse = lax.rsqrt(jnp.mean(mixed * mixed, axis=-1, keepdims=True) + norm_eps)
    normed = mixed * inverse
    out_ref[...] = normed.astype(BF16)
    up = up_ref[...].astype(F32)
    inner = jnp.mean(up * normed, axis=-1, keepdims=True)
    gm = ((up - normed * inner) * inverse).astype(BF16)
    gm_ref[...] = gm
    total = rows_by_rows(q, gm)
    total_ref[...] = total
    total16_ref[...] = total.astype(BF16)


def local_grad_kernel(
    blocks, q_ref, k_ref, v_ref, gm_ref, local_ref, prior_ref, gq_ref, gk_ref, gv_ref, gv16_ref
):
    mask = causal_mask()
    state = jnp.zeros((DK, DK), F32)
    for i in reversed(range(blocks)):
        q, k, v, gm = (ref[block_rows(i), :] for ref in (q_ref, k_ref, v_ref, gm_ref))
        scores = jnp.where(mask, by_rows(q, k), 0.0).astype(BF16)
        gscores = jnp.where(mask, by_rows(gm, v), 0.0).astype(BF16)
        later = state.astype(BF16)
        prior = (prior_ref[...] + local_ref[i].astype(F32)).astype(BF16)
        gq_ref[block_rows(i), :] = (plain(gscores, k) + by_rows(gm, prior)).astype(BF16)
        gk_ref[block_rows(i), :] = rows_by_rows(gscores, q) + by_rows(v, later)
        gv = rows_by_rows(scores, gm) + plain(k, later)
        gv_ref[block_rows(i), :] = gv
        gv16_ref[block_rows(i), :] = gv.astype(BF16)
        if i:
            state = state + rows_by_rows(q, gm)


def grad_key_kernel(gk_ref, v_ref, after_ref, out_ref):
    out_ref[...] = (gk_ref[...] + by_rows(v_ref[...], after_ref[...])).astype(BF16)


def latent_part(sent, piece_refs, g_ref, out_ref):
    _, pair, head = place()
    width = piece_refs[0].shape[1]
    rows = out_ref.shape[-1]
    chunks = width // rows
    odd = lax.rem(pair, 2) ^ sent
    for k in range(len(piece_refs) // 2):
        for c in range(0, chunks, 2):
            part = None
            for t in range(2):
                two = piece_refs[2 * k + t][:, c * rows : (c + 2) * rows]
                one = jnp.where(odd == 0, two[:, :rows], two[:, rows:])
                term = plain(g_ref[t], one)
                part = term if part is None else part + term
            slab = (head ^ k) * chunks + c + odd
            out_ref[lax.div(pair ^ slab, 2)] = part.astype(out_ref.dtype)


def latent_send_kernel(gv_ref, k_ref, after_ref, got_ref, k_got_ref, after_got_ref, *refs):
    piece_refs = refs[:-2]
    out_ref, g_ref = refs[-2:]
    side, _, _ = place()
    tokens = piece_refs[0].shape[0]
    after, after_got = after_ref[...], after_got_ref[...]
    for t in range(2):
        at = pl.ds(pl.multiple_of((side ^ t) * tokens, tokens), tokens)
        own = gv_ref[at, :] + plain(k_ref[at, :], after)
        got = got_ref[at, :].astype(F32) + plain(k_got_ref[at, :], after_got)
        g_ref[t, :DK, :] = jnp.where(side == 0, own, got).T.astype(BF16)
        g_ref[t, DK:, :] = jnp.where(side == 0, got, own).T.astype(BF16)
    latent_part(1, piece_refs, g_ref, out_ref)


def latent_keep_kernel(g_ref, *refs):
    latent_part(0, refs[:-1], g_ref, refs[-1])


def join_kernel(i, keep_ref, got_ref, out_ref):
    out_ref[...] = (keep_ref[i] + got_ref[...].astype(F32)).astype(BF16)


def sum_kernel(n, *refs):
    total = refs[0][0]
    for ref in refs[1:n]:
        total = total + ref[...].astype(F32)
    refs[n][...] = total.T


def in_hbm(array):
    return pltpu.with_memory_space_constraint(array, pltpu.HBM)


def pick(flag, even, odd):
    return jnp.where(flag == 0, even, odd)


def per_device(inputs, latent, queries, keys, grad_out):
    n, heads = lax.axis_size("seq"), lax.axis_size("head")
    side, pair, head = place()
    rows, columns = latent.shape
    tokens = inputs.shape[0]
    pairs, far = n // 2, n // 4
    blocks = 2 * tokens // BLOCK

    def half(flag):
        chunks = [
            pick(flag, inputs[:, 2 * c * rows :][:, :rows], inputs[:, (2 * c + 1) * rows :][:, :rows])
            for c in range(inputs.shape[1] // (2 * rows))
        ]
        return jnp.concatenate(chunks, axis=1)

    sums = jnp.sum(jnp.abs(latent), axis=0, keepdims=True)
    got_sums = swap(sums, "seq", 1)
    sent_half, got_sums = lax.optimization_barrier((half(1 - side), got_sums))
    got_half = swap(sent_half, "seq", 1)
    own_half = half(side)

    (slab,) = call(slab_kernel, [shape((rows + EXTRA, columns), BF16)], [latent, sums, got_sums], 0)
    even = [slab] + [None] * (far - 1)
    odd = [swap(slab, "seq", 2)] + [None] * (far - 1)
    for i in range(2, far):
        even[i] = swap(slab, "seq", 4 * i)
    if far > 1:
        even[1] = swap(slab, "seq", 4)
        held, odd[0] = lax.optimization_barrier((even[1], odd[0]))
        odd[1] = swap(held, "seq", 2)
    even[2:], odd[:2] = lax.optimization_barrier((even[2:], odd[:2]))
    for i in range(2, far):
        odd[i] = swap(even[i], "seq", 2)
    slab_list = even + odd
    own_late, _ = lax.optimization_barrier((own_half, even[-1]))
    own_pieces = [own_half] + [swap(own_late, "head", k) for k in range(1, heads)]
    half_cost = 2 * tokens * pairs * rows * columns
    weights, keep_own, send_own = call(
        functools.partial(project_own_kernel, far, len(slab_list), n * rows),
        [
            shape((pairs * rows, columns), BF16),
            shape((tokens, DK), F32),
            shape((tokens, DK), BF16),
        ],
        [in_hbm(a) for a in slab_list] + own_pieces,
        half_cost,
        [pltpu.VMEM((pairs, *slab.shape), BF16), pltpu.SemaphoreType.DMA((pairs,))],
        [pl.BlockSpec(memory_space=pl.ANY)] * pairs + vmem_specs(heads),
    )
    got_late, _ = lax.optimization_barrier((got_half, odd))
    keys_late, _ = lax.optimization_barrier((keys, even[-1]))
    got_pieces = [got_half] + [swap(got_late, "head", k) for k in range(1, heads)]
    keep_got, send_got = call(
        project_got_kernel,
        [shape((tokens, DK), F32), shape((tokens, DK), BF16)],
        [weights] + got_pieces,
        half_cost,
    )
    values_got, values_own = swap(send_own, "seq", 1), swap(send_got, "seq", 1)
    pieces = [a for two in zip(own_pieces, got_pieces) for a in two]

    def part_of(array, flag):
        return pick(flag, array[:, :DK], array[:, DK:])

    def joined(mine, theirs, late):
        mine, theirs, _ = lax.optimization_barrier((mine, theirs, late))
        return jnp.concatenate([pick(side, mine, theirs), pick(side, theirs, mine)], axis=0)

    k = joined(part_of(keys_late, side), swap(part_of(keys_late, 1 - side), "seq", 1), send_got)
    long = 2 * tokens
    cost = 2 * long * DK * DK
    v, total, total16 = call(
        values_kernel,
        [shape((long, DK), BF16), shape((DK, DK), F32), shape((DK, DK), BF16)],
        [keep_own, values_own, keep_got, values_got, k],
        cost,
    )
    parked = list(park(pieces, v))
    queries_late, up_late, keys_later, _ = lax.optimization_barrier(
        (queries, grad_out, keys, send_got)
    )
    early = [
        (part_of(a, side), swap(part_of(a, 1 - side), "seq", 1)) for a in (queries_late, up_late)
    ]
    k_parts = part_of(keys_later, 1 - side), swap(part_of(keys_later, side), "seq", 1)

    def scan(total, total16, backward, hooks):
        before = jnp.zeros_like(total)
        distance, at, results = 1, 0, []
        while distance < pairs:
            got = swap(total16, "seq", 2 * distance).astype(F32)
            high = lax.rem(lax.div(pair, distance), 2) == (0 if backward else 1)
            before = before + jnp.where(high, got, 0.0)
            if at < len(hooks):
                result = hooks[at](total16)
            total = total + got
            total16 = total.astype(BF16)
            if at < len(hooks):
                total16, result = lax.optimization_barrier((total16, result))
                results.append(result)
            distance, at = distance * 2, at + 1
        return before, results

    def intra():
        return call(
            functools.partial(intra_kernel, blocks),
            [shape((long, DK), F32), shape((blocks, DK, DK), BF16)],
            [q, k, v],
            4 * cost,
        )

    prior, (_, (pieces, (q, up))) = scan(
        total,
        total16,
        False,
        [lambda _: (), lambda late: (parked, [joined(*a, late) for a in early])],
    )
    mixed, local_prior = intra()
    out, gm, gtotal, gtotal16 = call(
        norm_kernel,
        [
            shape((long, DK), BF16),
            shape((long, DK), BF16),
            shape((DK, DK), F32),
            shape((DK, DK), BF16),
        ],
        [mixed, prior, q, up],
        2 * cost,
    )

    def local_grads():
        return call(
            functools.partial(local_grad_kernel, blocks),
            [
                shape((long, DK), BF16),
                shape((long, DK), F32),
                shape((long, DK), F32),
                shape((long, DK), BF16),
            ],
            [q, k, v, gm, local_prior, prior],
            9 * cost,
        )

    local = local_grads()
    after, ((_, (gq, gk_part, gv_part, gv16)), k_got) = scan(
        gtotal, gtotal16, True, [lambda _: ((), local), lambda late: joined(*k_parts, late)]
    )
    gv_got = swap(gv16, "seq", 1)
    after16 = after.astype(BF16)
    after16, gv_got = lax.optimization_barrier((after16, gv_got))
    after_got = swap(after16, "seq", 1)
    half_slabs = (far, columns, rows)
    send_parts, gv_both = call(
        latent_send_kernel,
        [shape(half_slabs, BF16), shape((2, columns, tokens), BF16)],
        [gv_part, k, after16, gv_got, k_got, after_got] + pieces,
        half_cost + 2 * cost,
    )
    (keep_parts,) = call(
        latent_keep_kernel, [shape(half_slabs, F32)], [gv_both] + pieces, half_cost
    )
    after_late, _ = lax.optimization_barrier((after16, send_parts))
    (gk,) = call(grad_key_kernel, [shape((long, DK), BF16)], [gk_part, v, after_late], cost)

    arrived = []
    for i in reversed(range(1, far)):
        got = swap(send_parts[i], "seq", 2)
        if arrived:
            got, _ = lax.optimization_barrier((got, joint))
        (joint,) = call(
            functools.partial(join_kernel, i), [shape((columns, rows), BF16)], [keep_parts, got], 0
        )
        arrived.append(swap(joint, "seq", 4 * i))
    terms = [keep_parts, swap(send_parts[0], "seq", 2)] + arrived
    def token_half(flag):
        return jnp.stack([pick(flag, a[:tokens], a[tokens:]) for a in (out, gq, gk)])

    mine, theirs = token_half(side), swap(token_half(1 - side), "seq", 1)
    attn_out, grad_queries, grad_keys = (
        jnp.concatenate([pick(side, mine[i], theirs[i]), pick(side, theirs[i], mine[i])], axis=1)
        for i in range(3)
    )
    outs, terms = lax.optimization_barrier(((attn_out, grad_queries, grad_keys), terms))
    (grad_latent,) = call(
        functools.partial(sum_kernel, len(terms)), [shape((rows, columns), F32)], terms, 0
    )
    return (*outs, grad_latent)


def solution(mesh):
    placed = (P("seq", "head"),) * 5
    return jax.shard_map(
        per_device,
        mesh=mesh,
        in_specs=placed,
        out_specs=(P("seq", "head"),) * 4,
        check_vma=False,
    )
```
